32 devices in a mesh: dp: 8 (over z, y), tensor: 4 (over x, core).
Axes of the slice: x: 2, y: 2, z: 4, core: 2. Of those that a mesh axis runs over, the one named last changes fastest.
Arguments:
- inputs: bfloat16 [32, 256, 1024], P('dp'), may hold values from -6 to 6
- cotangent: bfloat16 [32, 256, 1024], P('dp'), may hold values from -6 to 6
- lengths: int32 [32], P('dp'), may hold values from 1 to 256, as said below
- up_weight: bfloat16 [1024, 2048], P(None, 'tensor')
- down_weight: bfloat16 [2048, 1024], P('tensor')
- noise_up: float32 [1024, 2048], P(None, 'tensor'), may hold values from -16 to 16
- noise_down: float32 [2048, 1024], P('tensor'), may hold values from -16 to 16
Outputs:
- grad_up: float32 [1024, 2048], P(None, 'tensor')
- grad_down: float32 [2048, 1024], P('tensor')
- input_grad: bfloat16 [32, 256, 1024], P('dp', None, 'tensor')
The draws below stay inside these ranges and needn't reach their ends.
Inputs may be any that keep to these rules, and one draw needn't show every extreme that they name: `lengths`: positions at or beyond a user's length are padding.
All inputs are finite; a program needn't handle non-finite values.
Results may differ from the reference program's by a relative error of at most 0.009.
Values may be sent and summed in bfloat16 or wider, within the bound.
A program may use at most 128 MiB of HBM per device.

```python
import jax
import jax.numpy as jnp
from jax import lax

D = 1024
FF = 2048
S = 256
USERS = 32
N_TENSOR = 4


def draw_lengths(key, part):
    key = jax.random.fold_in(key, 3)
    first, second, third = jax.random.split(key, 3)
    top = S.bit_length() - 1
    power = jax.random.randint(first, (USERS,), 0, top + 1)
    base = jnp.left_shift(jnp.ones((USERS,), jnp.int32), power.astype(jnp.int32))
    extra = jax.random.randint(second, (USERS,), 0, base)
    lengths = jnp.minimum(base + extra, S).astype(jnp.int32)
    pick = jax.random.randint(third, (), 0, USERS)
    return lengths.at[pick].set(S).astype(jnp.int32)


def ramped_normal(key, rows, cols, along_rows, steep, fan_in):
    values = jax.random.normal(key, (rows, cols), jnp.float32)
    count = rows if along_rows else cols
    ramp = steep ** (jnp.arange(count, dtype=jnp.float32) / count - 0.5)
    ramp = ramp[:, None] if along_rows else ramp[None, :]
    return values * ramp / jnp.sqrt(jnp.float32(fan_in))


def draw_up_weight(key, part):
    key = jax.random.fold_in(key, 11)
    return ramped_normal(key, D, FF, False, 3.0, D).astype(jnp.bfloat16)


def draw_down_weight(key, part):
    key = jax.random.fold_in(key, 17)
    return ramped_normal(key, FF, D, True, 3.0, FF).astype(jnp.bfloat16)


def block_levels(own_key, shape, cuts, least, high):
    level, own = 1.0, jax.random.fold_in(own_key, 6)
    for axis_at, blocks in cuts:
        steps = jnp.exp(jax.random.uniform(jax.random.fold_in(own, axis_at), (blocks,), jnp.float32, least / len(cuts), high / len(cuts)))
        level = level * jnp.repeat(steps, shape[axis_at] // blocks).reshape([-1 if axis == axis_at else 1 for axis in range(len(shape))])
    return level


def noise(key, dims, width, reach, cuts=(), held_as=jnp.bfloat16):
    array = width * jax.random.normal(key, dims, jnp.float32)
    if cuts:
        array = array * block_levels(key, dims, cuts, -0.22, 0.18)
    return jnp.clip(array, -reach, reach).astype(held_as)


def setup_inputs(seed: int = 0) -> dict:
    seeds = jax.random.split(jax.random.key(seed), 8)
    return {
        "inputs": noise(seeds[0], (USERS, S, D), 1.0, 6.0, ((0, 8),)),
        "cotangent": noise(seeds[1], (USERS, S, D), 1.0, 6.0, ((0, 8),)),
        "lengths": draw_lengths(jax.random.fold_in(seeds[7], 71), 0),
        "up_weight": draw_up_weight(jax.random.fold_in(seeds[7], 71), 0),
        "down_weight": draw_down_weight(jax.random.fold_in(seeds[7], 71), 0),
        "noise_up": noise(seeds[5], (D, FF), 3.0, 16.0, ((1, 4),), jnp.float32),
        "noise_down": noise(seeds[6], (FF, D), 3.0, 16.0, ((0, 4),), jnp.float32),
    }


clip_scale = 0.25
norm_epsilon = 1e-06

def gelu_slope(pre, back):
    return jax.vjp(jax.nn.gelu, pre)[1](back)[0]

def reference(inputs, cotangent, lengths, up_weight, down_weight, noise_up, noise_down):
    positions = jnp.arange(S, dtype=jnp.int32)
    block = FF // N_TENSOR
    clip_bound = jnp.float32(clip_scale * (D * FF) ** 0.5)

    def member(carry, items):
        acc_up, acc_down = carry
        tokens, grads, length = items
        mask = (positions < length)[:, None]
        masked = jnp.where(mask, grads, jnp.zeros_like(grads))
        pre = jnp.dot(tokens, up_weight, preferred_element_type=jnp.float32)
        active = jax.nn.gelu(pre).astype(jnp.bfloat16)
        back = jnp.dot(masked, down_weight.T, preferred_element_type=jnp.float32)
        slopes = gelu_slope(pre, back).astype(jnp.bfloat16)
        parts = jnp.einsum('skf,dkf->ksd', slopes.astype(jnp.float32).reshape(S, N_TENSOR, block), up_weight.astype(jnp.float32).reshape(D, N_TENSOR, block), precision=lax.Precision.HIGHEST)
        rounded = lax.optimization_barrier(parts.astype(jnp.bfloat16)).astype(jnp.float32)
        token_grad = lax.optimization_barrier(jnp.sum(rounded, axis=0)).astype(jnp.bfloat16)
        down_each = jnp.dot(active.T, masked, preferred_element_type=jnp.float32)
        up_each = jnp.dot(tokens.T, slopes, preferred_element_type=jnp.float32)
        squares = jnp.sum(up_each * up_each) + jnp.sum(down_each * down_each)
        factor = jnp.minimum(jnp.float32(1.0), clip_bound / jnp.sqrt(squares + norm_epsilon))
        return ((acc_up + factor * up_each, acc_down + factor * down_each), token_grad)
    start = (jnp.zeros((D, FF), jnp.float32), jnp.zeros((FF, D), jnp.float32))
    (sum_up, sum_down), input_grad = lax.scan(member, start, (inputs, cotangent, lengths))
    grad_up = sum_up + noise_up
    grad_down = sum_down + noise_down
    return (grad_up, grad_down, input_grad)
```

```python
import functools

import jax
import jax.numpy as jnp
from jax import lax
from jax.experimental import pallas as pl
from jax.experimental.pallas import tpu as pltpu
from jax.sharding import PartitionSpec as P

clip_scale = 0.25
norm_epsilon = 1e-06
ROWS = 256
CHUNK_COLS = 512
GELU_C = 0.7978845608028654
GELU_A = 0.044715
MESH_IDS = pl.DeviceIdType.MESH
F32 = jnp.float32
BF16 = jnp.bfloat16


def dot(a, b, ca, cb):
    return lax.dot_general(a, b, (((ca,), (cb,)), ((), ())), preferred_element_type=F32)


def kernel(
    n_dp, n_tensor, bound,
    lengths, x_ref, c_ref, wu_ref, wd_ref,
    up_out, down_out, tok_out,
    masked, act, slopes, token, token_in, squares, acc, gathered, *rest,
):
    levels = n_dp.bit_length() - 1
    outgoing, incoming = rest[:levels], rest[levels : 2 * levels]
    (sq_send, sq_recv, tok_send, tok_recv, red_send, red_recv, gat_send, gat_recv,
     out_sem) = rest[2 * levels :]
    users, seq, d = x_ref.shape
    f = wu_ref.shape[1]
    own_cols = d // n_tensor
    n_up = d // ROWS
    down_split = d // CHUNK_COLS
    n_chunks = acc.shape[0]
    me_dp = lax.axis_index("dp")
    me_t = lax.axis_index("tensor")

    def peer(j):
        return lax.rem(me_t + j, n_tensor)

    def slot_from(j):
        return n_tensor - j - 1

    bits, partners, offsets, others = [], [], [0], []
    for k in range(levels):
        count = ROWS >> (k + 1)
        bit = lax.rem(me_dp // (1 << k), 2)
        bits.append(bit)
        partners.append(me_dp + (1 - 2 * bit) * (1 << k))
        offsets.append(offsets[-1] + bit * count)
        others.append(offsets[-2] + (1 - bit) * count)

    barrier = pltpu.get_barrier_semaphore()
    for j in range(1, n_tensor):
        pl.semaphore_signal(barrier, inc=1, device_id=(me_dp, peer(j)), device_id_type=MESH_IDS)
    for k in range(levels):
        pl.semaphore_signal(barrier, inc=1, device_id=(partners[k], me_t), device_id_type=MESH_IDS)

    def first(u, carry):
        tokens = x_ref[u]
        pos = lax.broadcasted_iota(jnp.int32, (seq, d), 0)
        grads = jnp.where(pos < lengths[u], c_ref[u].astype(F32), 0.0).astype(BF16)
        masked[u] = grads
        pre = dot(tokens, wu_ref[...], 1, 0)
        back = dot(grads, wd_ref[...], 1, 1)
        sq = pre * pre
        t = jnp.tanh(GELU_C * (pre + GELU_A * (sq * pre)))
        half = 0.5 * (1.0 + t)
        a = (pre * half).astype(BF16)
        slope = half + 0.5 * pre * (1.0 - t * t) * (GELU_C * (1.0 + 3.0 * GELU_A * sq))
        s = (back * slope).astype(BF16)
        act[u] = a
        slopes[u] = s
        terms = dot(tokens, tokens, 1, 1) * dot(s, s, 1, 1)
        terms += dot(grads, grads, 1, 1) * dot(a, a, 1, 1)
        total = jnp.sum(jnp.sum(terms, axis=0, keepdims=True), axis=1, keepdims=True)
        squares[0, u] = jnp.broadcast_to(total, (8, 128))
        return carry

    lax.fori_loop(0, users, first, 0)

    pl.semaphore_wait(barrier, n_tensor - 1 + levels)

    def square_copy(j):
        return pltpu.make_async_remote_copy(
            src_ref=squares.at[0], dst_ref=squares.at[j],
            send_sem=sq_send.at[j - 1], recv_sem=sq_recv.at[j - 1],
            device_id=(me_dp, peer(j)), device_id_type=MESH_IDS,
        )

    for j in range(1, n_tensor):
        square_copy(j).start()

    def token_terms(u, carry):
        t = dot(slopes[u], wu_ref[...], 1, 1).astype(BF16)
        for k in range(n_tensor):
            token[k, u] = t[:, k * own_cols : (k + 1) * own_cols]
        return carry

    lax.fori_loop(0, users, token_terms, 0)

    def token_copy(j):
        return pltpu.make_async_remote_copy(
            src_ref=token.at[peer(j)], dst_ref=token_in.at[j - 1],
            send_sem=tok_send.at[j - 1], recv_sem=tok_recv.at[j - 1],
            device_id=(me_dp, peer(j)), device_id_type=MESH_IDS,
        )

    for j in range(1, n_tensor):
        token_copy(j).start()

    for j in range(1, n_tensor):
        square_copy(j).wait()
    total_sq = squares[0]
    for j in range(1, n_tensor):
        total_sq += squares[j]
    factors = jnp.minimum(1.0, bound / jnp.sqrt(jnp.maximum(total_sq, 0.0) + norm_epsilon))
    scale = [factors[u, 0:1, 0:1] for u in range(users)]

    def reduce_copy(c, k):
        return pltpu.make_async_remote_copy(
            src_ref=outgoing[k].at[c], dst_ref=incoming[k].at[c],
            send_sem=red_send.at[k, c], recv_sem=red_recv.at[k, c],
            device_id=(partners[k], me_t), device_id_type=MESH_IDS,
        )

    def gather_copy(c, k):
        count = ROWS >> (k + 1)
        rows = pl.ds(pl.multiple_of(offsets[k + 1], count), count)
        return pltpu.make_async_remote_copy(
            src_ref=gathered.at[c, rows], dst_ref=gathered.at[c, rows],
            send_sem=gat_send.at[k, c], recv_sem=gat_recv.at[k, c],
            device_id=(partners[k], me_t), device_id_type=MESH_IDS,
        )

    def send_half(c, k):
        count = ROWS >> (k + 1)
        outgoing[k][c] = acc[c, pl.ds(pl.multiple_of(others[k], count), count)].astype(BF16)
        reduce_copy(c, k).start()

    def up_chunk(i, carry):
        cols = pl.ds(pl.multiple_of(i * ROWS, ROWS), ROWS)
        value = scale[0] * dot(x_ref[0, :, cols], slopes[0], 0, 0)
        for u in range(1, users):
            value += scale[u] * dot(x_ref[u, :, cols], slopes[u], 0, 0)
        acc[i] = value
        send_half(i, 0)
        return carry

    def down_chunk(i, carry):
        rows = pl.ds(pl.multiple_of((i // down_split) * ROWS, ROWS), ROWS)
        cols = pl.ds(pl.multiple_of((i % down_split) * CHUNK_COLS, CHUNK_COLS), CHUNK_COLS)
        value = scale[0] * dot(act[0, :, rows], masked[0, :, cols], 0, 0)
        for u in range(1, users):
            value += scale[u] * dot(act[u, :, rows], masked[u, :, cols], 0, 0)
        acc[n_up + i] = value
        send_half(n_up + i, 0)
        return carry

    lax.fori_loop(0, n_up, up_chunk, 0)
    lax.fori_loop(0, n_chunks - n_up, down_chunk, 0)

    def up_copy(c):
        return pltpu.make_async_copy(
            gathered.at[c], up_out.at[pl.ds(pl.multiple_of(c * ROWS, ROWS), ROWS)], out_sem.at[c]
        )

    def down_copy(c):
        i = c - n_up
        rows = pl.ds(pl.multiple_of((i // down_split) * ROWS, ROWS), ROWS)
        cols = pl.ds(pl.multiple_of((i % down_split) * CHUNK_COLS, CHUNK_COLS), CHUNK_COLS)
        return pltpu.make_async_copy(gathered.at[c], down_out.at[rows, cols], out_sem.at[c])

    def stage(c, s):
        if s < levels:
            k = s
            count = ROWS >> (k + 1)
            mine = pl.ds(pl.multiple_of(offsets[k + 1], count), count)
            reduce_copy(c, k).wait()
            acc[c, mine] += incoming[k][c].astype(F32)
            if k + 1 < levels:
                send_half(c, k + 1)
            else:
                gathered[c, mine] = acc[c, mine].astype(BF16)
                gather_copy(c, k).start()
        else:
            k = 2 * levels - 1 - s
            gather_copy(c, k).wait()
            if k > 0:
                gather_copy(c, k - 1).start()
            else:
                @pl.when(c < n_up)
                def _():
                    up_copy(c).start()

                @pl.when(c >= n_up)
                def _():
                    down_copy(c).start()

    def slot(t, carry):
        for s in reversed(range(2 * levels)):
            @pl.when((t >= s) & (t - s < n_chunks))
            def _():
                stage(t - s, s)
        return carry

    lax.fori_loop(0, n_chunks + 2 * levels - 1, slot, 0)

    for j in range(1, n_tensor):
        token_copy(j).wait()

    def finish(u, carry):
        total = token[me_t, u].astype(F32)
        for j in range(1, n_tensor):
            total += token_in[j - 1, u].astype(F32)
        tok_out[u] = total.astype(BF16)
        return carry

    lax.fori_loop(0, users, finish, 0)

    lax.fori_loop(0, n_up, lambda c, carry: (up_copy(c).wait(), carry)[1], 0)
    lax.fori_loop(n_up, n_chunks, lambda c, carry: (down_copy(c).wait(), carry)[1], 0)


def fused(n_dp, n_tensor, inputs, cotangent, lengths, up_weight, down_weight, noise_up, noise_down):
    users, seq, d = inputs.shape
    f = up_weight.shape[1]
    bound = clip_scale * (d * f * n_tensor) ** 0.5
    levels = n_dp.bit_length() - 1
    n_chunks = d // ROWS + (f // ROWS) * (d // CHUNK_COLS)
    own = d // n_tensor
    vmem = pl.BlockSpec(memory_space=pltpu.VMEM)
    smem = pl.BlockSpec(memory_space=pltpu.SMEM)
    anyspace = pl.BlockSpec(memory_space=pl.ANY)
    halves = [pltpu.VMEM((n_chunks, ROWS >> (k + 1), CHUNK_COLS), BF16) for k in range(levels)]
    sem = pltpu.SemaphoreType.DMA
    total_up, total_down, input_grad = pl.pallas_call(
        functools.partial(kernel, n_dp, n_tensor, bound),
        out_shape=(
            jax.ShapeDtypeStruct((d, f), BF16),
            jax.ShapeDtypeStruct((f, d), BF16),
            jax.ShapeDtypeStruct((users, seq, own), BF16),
        ),
        in_specs=[smem, vmem, vmem, vmem, vmem],
        out_specs=(anyspace, anyspace, vmem),
        scratch_shapes=[
            pltpu.VMEM((users, seq, d), BF16),
            pltpu.VMEM((users, seq, f), BF16),
            pltpu.VMEM((users, seq, f), BF16),
            pltpu.VMEM((n_tensor, users, seq, own), BF16),
            pltpu.VMEM((n_tensor - 1, users, seq, own), BF16),
            pltpu.VMEM((n_tensor, users, 8, 128), F32),
            pltpu.VMEM((n_chunks, ROWS, CHUNK_COLS), F32),
            pltpu.VMEM((n_chunks, ROWS, CHUNK_COLS), BF16),
            *halves,
            *halves,
            sem((n_tensor - 1,)), sem((n_tensor - 1,)),
            sem((n_tensor - 1,)), sem((n_tensor - 1,)),
            sem((levels, n_chunks)), sem((levels, n_chunks)),
            sem((levels, n_chunks)), sem((levels, n_chunks)),
            sem((n_chunks,)),
        ],
        compiler_params=pltpu.CompilerParams(
            collective_id=0, has_side_effects=True, vmem_limit_bytes=48 * 1024 * 1024
        ),
    )(lengths, inputs, cotangent, up_weight, down_weight)
    return (
        total_up.astype(F32) + noise_up,
        total_down.astype(F32) + noise_down,
        input_grad,
    )


def gelu_slope(pre, back):
    return jax.vjp(jax.nn.gelu, pre)[1](back)[0]


def plain(n_tensor, inputs, cotangent, lengths, up_weight, down_weight, noise_up, noise_down):
    members, seq, d = inputs.shape
    bound = F32(clip_scale * (d * up_weight.shape[1] * n_tensor) ** 0.5)
    positions = lax.broadcasted_iota(jnp.int32, (members, seq), 1)
    mask = (positions < lengths[:, None])[:, :, None]
    masked = jnp.where(mask, cotangent, jnp.zeros_like(cotangent))
    pre = jnp.einsum("usd,df->usf", inputs, up_weight, preferred_element_type=F32)
    active = jax.nn.gelu(pre).astype(BF16)
    back = jnp.einsum("usd,fd->usf", masked, down_weight, preferred_element_type=F32)
    slopes = gelu_slope(pre, back).astype(BF16)
    token_terms = jnp.einsum("usf,df->usd", slopes, up_weight, preferred_element_type=F32)
    input_grad = lax.psum_scatter(
        token_terms.astype(BF16), "tensor", scatter_dimension=2, tiled=True
    )
    down_each = jnp.einsum("usf,usd->ufd", active, masked, preferred_element_type=F32)
    up_each = jnp.einsum("usd,usf->udf", inputs, slopes, preferred_element_type=F32)
    partial_sq = jnp.sum(down_each * down_each, axis=(1, 2)) + jnp.sum(
        up_each * up_each, axis=(1, 2)
    )
    squares = lax.psum(partial_sq, "tensor")
    factors = jnp.minimum(F32(1.0), bound / jnp.sqrt(squares + norm_epsilon))
    sum_down = jnp.sum(factors[:, None, None] * down_each, axis=0)
    sum_up = jnp.sum(factors[:, None, None] * up_each, axis=0)
    total_up, total_down = lax.psum((sum_up, sum_down), "dp")
    return (total_up + noise_up, total_down + noise_down, input_grad)


def solution(mesh):
    n_dp, n_tensor = mesh.shape["dp"], mesh.shape["tensor"]

    def per_device(*args):
        d, f = args[3].shape
        fits = n_dp & (n_dp - 1) == 0 and 2 <= n_dp <= ROWS // 16 and n_tensor > 1
        fits = fits and f == CHUNK_COLS and d % CHUNK_COLS == 0 and (d // n_tensor) % 128 == 0
        if fits:
            return fused(n_dp, n_tensor, *args)
        return plain(n_tensor, *args)

    placed = (
        P("dp", None, None),
        P("dp", None, None),
        P("dp"),
        P(None, "tensor"),
        P("tensor", None),
        P(None, "tensor"),
        P("tensor", None),
    )
    return jax.shard_map(
        per_device,
        mesh=mesh,
        in_specs=placed,
        out_specs=(P(None, "tensor"), P("tensor", None), P("dp", None, "tensor")),
        check_vma=False,
    )
```

```python
import functools

import jax
import jax.numpy as jnp
from jax import lax
from jax.experimental import pallas as pl
from jax.experimental.pallas import tpu as pltpu
from jax.sharding import PartitionSpec as P

clip_scale = 0.25
norm_epsilon = 1e-06
ROWS = 256
CHUNK_COLS = 512
AHEAD = 1
GELU_C = 0.7978845608028654
GELU_A = 0.044715
MESH_IDS = pl.DeviceIdType.MESH
F32 = jnp.float32
BF16 = jnp.bfloat16


def dot(a, b, ca, cb):
    return lax.dot_general(a, b, (((ca,), (cb,)), ((), ())), preferred_element_type=F32)


def kernel(
    n_dp, n_tensor, bound,
    lengths, x_ref, c_ref, wu_ref, wd_ref,
    up_out, down_out, tok_out,
    masked, act, slopes, token, token_in, squares, acc, gathered, *rest,
):
    levels = n_dp.bit_length() - 1
    outgoing, incoming = rest[:levels], rest[levels : 2 * levels]
    (sq_send, sq_recv, tok_send, tok_recv, red_send, red_recv, gat_send, gat_recv,
     out_sem) = rest[2 * levels :]
    users, seq, d = x_ref.shape
    f = wu_ref.shape[1]
    own_cols = d // n_tensor
    n_up = d // ROWS
    down_split = d // CHUNK_COLS
    n_chunks = acc.shape[0]
    me_dp = lax.axis_index("dp")
    me_t = lax.axis_index("tensor")

    def peer(j):
        return lax.rem(me_t + j, n_tensor)

    def slot_from(j):
        return n_tensor - j - 1

    bits = [lax.rem(me_dp // (1 << k), 2) for k in range(levels)]
    across = [me_dp + (1 - 2 * bits[k]) * (1 << k) for k in range(levels)]
    offsets, others = [0], []
    for k in range(levels):
        count = ROWS >> (k + 1)
        others.append(offsets[-1] + (1 - bits[k]) * count)
        offsets.append(offsets[-1] + bits[k] * count)
    plan = (across, offsets, others)

    barrier = pltpu.get_barrier_semaphore()
    for j in range(1, n_tensor):
        pl.semaphore_signal(barrier, inc=1, device_id=(me_dp, peer(j)), device_id_type=MESH_IDS)
    for k in range(levels):
        pl.semaphore_signal(barrier, inc=1, device_id=(across[k], me_t), device_id_type=MESH_IDS)

    def first(u, carry):
        tokens = x_ref[u]
        pos = lax.broadcasted_iota(jnp.int32, (seq, d), 0)
        grads = jnp.where(pos < lengths[u], c_ref[u].astype(F32), 0.0).astype(BF16)
        masked[u] = grads
        pre = dot(tokens, wu_ref[...], 1, 0)
        back = dot(grads, wd_ref[...], 1, 1)
        sq = pre * pre
        t = jnp.tanh(GELU_C * (pre + GELU_A * (sq * pre)))
        half = 0.5 * (1.0 + t)
        a = (pre * half).astype(BF16)
        slope = half + 0.5 * pre * (1.0 - t * t) * (GELU_C * (1.0 + 3.0 * GELU_A * sq))
        s = (back * slope).astype(BF16)
        act[u] = a
        slopes[u] = s
        terms = dot(tokens, tokens, 1, 1) * dot(s, s, 1, 1)
        terms += dot(grads, grads, 1, 1) * dot(a, a, 1, 1)
        total = jnp.sum(jnp.sum(terms, axis=0, keepdims=True), axis=1, keepdims=True)
        squares[0, u] = jnp.broadcast_to(total, (8, 128))
        return carry

    lax.fori_loop(0, users, first, 0)

    pl.semaphore_wait(barrier, n_tensor - 1 + levels)

    def square_copy(j):
        return pltpu.make_async_remote_copy(
            src_ref=squares.at[0], dst_ref=squares.at[j],
            send_sem=sq_send.at[j - 1], recv_sem=sq_recv.at[j - 1],
            device_id=(me_dp, peer(j)), device_id_type=MESH_IDS,
        )

    for j in range(1, n_tensor):
        square_copy(j).start()

    def token_terms(u, carry):
        t = dot(slopes[u], wu_ref[...], 1, 1).astype(BF16)
        for k in range(n_tensor):
            token[k, u] = t[:, k * own_cols : (k + 1) * own_cols]
        return carry

    lax.fori_loop(0, users, token_terms, 0)

    def token_copy(j):
        return pltpu.make_async_remote_copy(
            src_ref=token.at[peer(j)], dst_ref=token_in.at[j - 1],
            send_sem=tok_send.at[j - 1], recv_sem=tok_recv.at[j - 1],
            device_id=(me_dp, peer(j)), device_id_type=MESH_IDS,
        )

    for j in range(1, n_tensor):
        token_copy(j).start()

    for j in range(1, n_tensor):
        square_copy(j).wait()
    total_sq = squares[0]
    for j in range(1, n_tensor):
        total_sq += squares[j]
    factors = jnp.minimum(1.0, bound / jnp.sqrt(jnp.maximum(total_sq, 0.0) + norm_epsilon))
    scale = [factors[u, 0:1, 0:1] for u in range(users)]

    def reduce_copy(plan, c, k):
        return pltpu.make_async_remote_copy(
            src_ref=outgoing[k].at[c], dst_ref=incoming[k].at[c],
            send_sem=red_send.at[k, c], recv_sem=red_recv.at[k, c],
            device_id=(plan[0][k], me_t), device_id_type=MESH_IDS,
        )

    def gather_copy(plan, c, k):
        count = ROWS >> (k + 1)
        rows = pl.ds(pl.multiple_of(plan[1][k + 1], count), count)
        return pltpu.make_async_remote_copy(
            src_ref=gathered.at[c, rows], dst_ref=gathered.at[c, rows],
            send_sem=gat_send.at[k, c], recv_sem=gat_recv.at[k, c],
            device_id=(plan[0][k], me_t), device_id_type=MESH_IDS,
        )

    def send_half(plan, c, k):
        count = ROWS >> (k + 1)
        outgoing[k][c] = acc[c, pl.ds(pl.multiple_of(plan[2][k], count), count)].astype(BF16)
        reduce_copy(plan, c, k).start()

    def up_chunk(i):
        cols = pl.ds(pl.multiple_of(i * ROWS, ROWS), ROWS)
        value = scale[0] * dot(x_ref[0, :, cols], slopes[0], 0, 0)
        for u in range(1, users):
            value += scale[u] * dot(x_ref[u, :, cols], slopes[u], 0, 0)
        acc[i] = value
        send_half(plan, i, 0)

    def down_chunk(i):
        rows = pl.ds(pl.multiple_of((i // down_split) * ROWS, ROWS), ROWS)
        cols = pl.ds(pl.multiple_of((i % down_split) * CHUNK_COLS, CHUNK_COLS), CHUNK_COLS)
        value = scale[0] * dot(act[0, :, rows], masked[0, :, cols], 0, 0)
        for u in range(1, users):
            value += scale[u] * dot(act[u, :, rows], masked[u, :, cols], 0, 0)
        acc[n_up + i] = value
        send_half(plan, n_up + i, 0)

    def produce(c):
        @pl.when(c < n_up)
        def _():
            up_chunk(c)

        @pl.when(c >= n_up)
        def _():
            down_chunk(c - n_up)

    def up_copy(c):
        return pltpu.make_async_copy(
            gathered.at[c], up_out.at[pl.ds(pl.multiple_of(c * ROWS, ROWS), ROWS)], out_sem.at[c]
        )

    def down_copy(c):
        i = c - n_up
        rows = pl.ds(pl.multiple_of((i // down_split) * ROWS, ROWS), ROWS)
        cols = pl.ds(pl.multiple_of((i % down_split) * CHUNK_COLS, CHUNK_COLS), CHUNK_COLS)
        return pltpu.make_async_copy(gathered.at[c], down_out.at[rows, cols], out_sem.at[c])

    def stage(plan, c, s):
        if s < levels:
            k = s
            count = ROWS >> (k + 1)
            mine = pl.ds(pl.multiple_of(plan[1][k + 1], count), count)
            reduce_copy(plan, c, k).wait()
            acc[c, mine] += incoming[k][c].astype(F32)
            if k + 1 < levels:
                send_half(plan, c, k + 1)
            else:
                gathered[c, mine] = acc[c, mine].astype(BF16)
                gather_copy(plan, c, k).start()
        else:
            k = 2 * levels - 1 - s
            gather_copy(plan, c, k).wait()
            if k > 0:
                gather_copy(plan, c, k - 1).start()

    def copy_out(c, wait):
        @pl.when(c < n_up)
        def _():
            copy = up_copy(c)
            copy.wait() if wait else copy.start()

        @pl.when(c >= n_up)
        def _():
            copy = down_copy(c)
            copy.wait() if wait else copy.start()

    def prime(c, carry):
        produce(c)
        return carry

    lax.fori_loop(0, AHEAD, prime, 0)

    def slot(t, carry):
        @pl.when(t + AHEAD < n_chunks)
        def _():
            produce(t + AHEAD)

        for s in reversed(range(2 * levels - 1)):
            @pl.when((t >= s) & (t - s < n_chunks))
            def _():
                stage(plan, t - s, s)
        return carry

    lax.fori_loop(0, n_chunks + 2 * levels - 2, slot, 0)

    def last(c, carry):
        stage(plan, c, 2 * levels - 1)
        copy_out(c, False)
        return carry

    for j in range(1, n_tensor):
        token_copy(j).wait()

    def finish(u, carry):
        total = token[me_t, u].astype(F32)
        for j in range(1, n_tensor):
            total += token_in[j - 1, u].astype(F32)
        tok_out[u] = total.astype(BF16)
        return carry

    lax.fori_loop(0, users, finish, 0)
    lax.fori_loop(0, n_chunks, last, 0)

    def drain(c, carry):
        copy_out(c, True)
        return carry

    lax.fori_loop(0, n_chunks, drain, 0)


def fused(n_dp, n_tensor, inputs, cotangent, lengths, up_weight, down_weight, noise_up, noise_down):
    users, seq, d = inputs.shape
    f = up_weight.shape[1]
    bound = clip_scale * (d * f * n_tensor) ** 0.5
    levels = n_dp.bit_length() - 1
    n_chunks = d // ROWS + (f // ROWS) * (d // CHUNK_COLS)
    own = d // n_tensor
    vmem = pl.BlockSpec(memory_space=pltpu.VMEM)
    smem = pl.BlockSpec(memory_space=pltpu.SMEM)
    anyspace = pl.BlockSpec(memory_space=pl.ANY)
    halves = [pltpu.VMEM((n_chunks, ROWS >> (k + 1), CHUNK_COLS), BF16) for k in range(levels)]
    sem = pltpu.SemaphoreType.DMA
    total_up, total_down, input_grad = pl.pallas_call(
        functools.partial(kernel, n_dp, n_tensor, bound),
        out_shape=(
            jax.ShapeDtypeStruct((d, f), BF16),
            jax.ShapeDtypeStruct((f, d), BF16),
            jax.ShapeDtypeStruct((users, seq, own), BF16),
        ),
        in_specs=[smem, vmem, vmem, vmem, vmem],
        out_specs=(anyspace, anyspace, vmem),
        scratch_shapes=[
            pltpu.VMEM((users, seq, d), BF16),
            pltpu.VMEM((users, seq, f), BF16),
            pltpu.VMEM((users, seq, f), BF16),
            pltpu.VMEM((n_tensor, users, seq, own), BF16),
            pltpu.VMEM((n_tensor - 1, users, seq, own), BF16),
            pltpu.VMEM((n_tensor, users, 8, 128), F32),
            pltpu.VMEM((n_chunks, ROWS, CHUNK_COLS), F32),
            pltpu.VMEM((n_chunks, ROWS, CHUNK_COLS), BF16),
            *halves,
            *halves,
            sem((n_tensor - 1,)), sem((n_tensor - 1,)),
            sem((n_tensor - 1,)), sem((n_tensor - 1,)),
            sem((levels, n_chunks)), sem((levels, n_chunks)),
            sem((levels, n_chunks)), sem((levels, n_chunks)),
            sem((n_chunks,)),
        ],
        compiler_params=pltpu.CompilerParams(
            collective_id=0, has_side_effects=True, vmem_limit_bytes=48 * 1024 * 1024
        ),
    )(lengths, inputs, cotangent, up_weight, down_weight)
    return (
        total_up.astype(F32) + noise_up,
        total_down.astype(F32) + noise_down,
        input_grad,
    )


def gelu_slope(pre, back):
    return jax.vjp(jax.nn.gelu, pre)[1](back)[0]


def plain(n_tensor, inputs, cotangent, lengths, up_weight, down_weight, noise_up, noise_down):
    members, seq, d = inputs.shape
    bound = F32(clip_scale * (d * up_weight.shape[1] * n_tensor) ** 0.5)
    positions = lax.broadcasted_iota(jnp.int32, (members, seq), 1)
    mask = (positions < lengths[:, None])[:, :, None]
    masked = jnp.where(mask, cotangent, jnp.zeros_like(cotangent))
    pre = jnp.einsum("usd,df->usf", inputs, up_weight, preferred_element_type=F32)
    active = jax.nn.gelu(pre).astype(BF16)
    back = jnp.einsum("usd,fd->usf", masked, down_weight, preferred_element_type=F32)
    slopes = gelu_slope(pre, back).astype(BF16)
    token_terms = jnp.einsum("usf,df->usd", slopes, up_weight, preferred_element_type=F32)
    input_grad = lax.psum_scatter(
        token_terms.astype(BF16), "tensor", scatter_dimension=2, tiled=True
    )
    down_each = jnp.einsum("usf,usd->ufd", active, masked, preferred_element_type=F32)
    up_each = jnp.einsum("usd,usf->udf", inputs, slopes, preferred_element_type=F32)
    partial_sq = jnp.sum(down_each * down_each, axis=(1, 2)) + jnp.sum(
        up_each * up_each, axis=(1, 2)
    )
    squares = lax.psum(partial_sq, "tensor")
    factors = jnp.minimum(F32(1.0), bound / jnp.sqrt(squares + norm_epsilon))
    sum_down = jnp.sum(factors[:, None, None] * down_each, axis=0)
    sum_up = jnp.sum(factors[:, None, None] * up_each, axis=0)
    total_up, total_down = lax.psum((sum_up, sum_down), "dp")
    return (total_up + noise_up, total_down + noise_down, input_grad)


def solution(mesh):
    n_dp, n_tensor = mesh.shape["dp"], mesh.shape["tensor"]

    def per_device(*args):
        d, f = args[3].shape
        fits = n_dp & (n_dp - 1) == 0 and 2 <= n_dp <= ROWS // 16 and n_tensor > 1
        fits = fits and f == CHUNK_COLS and d % CHUNK_COLS == 0 and (d // n_tensor) % 128 == 0
        if fits:
            return fused(n_dp, n_tensor, *args)
        return plain(n_tensor, *args)

    placed = (
        P("dp", None, None),
        P("dp", None, None),
        P("dp"),
        P(None, "tensor"),
        P("tensor", None),
        P(None, "tensor"),
        P("tensor", None),
    )
    return jax.shard_map(
        per_device,
        mesh=mesh,
        in_specs=placed,
        out_specs=(P(None, "tensor"), P("tensor", None), P("dp", None, "tensor")),
        check_vma=False,
    )
```
